128 devices in a mesh: row: 8 (over z, core), col: 16 (over y, x).
Axes of the slice: x: 4, y: 4, z: 4, core: 2. Of those that a mesh axis runs over, the one named last changes fastest.
Arguments:
- tokens: bfloat16 [128, 8192], P('row', 'col'), may hold values from -6 to 6
- gate_weight: bfloat16 [8192, 26624], P('col', 'row'), may hold values from -0.0625 to 0.0625
- up_weight: bfloat16 [8192, 26624], P('col', 'row'), may hold values from -0.0625 to 0.0625
- down_weight: bfloat16 [26624, 8192], P('row', 'col'), may hold values from -0.0390625 to 0.0390625
- gate_tangent: bfloat16 [8192, 26624], P('col', 'row'), may hold values from -0.0625 to 0.0625
- up_tangent: bfloat16 [8192, 26624], P('col', 'row'), may hold values from -0.0625 to 0.0625
Outputs:
- gate_product: bfloat16 [8192, 26624], P('col', 'row')
- up_product: bfloat16 [8192, 26624], P('col', 'row')
The draws below stay inside these ranges and needn't reach their ends.
All inputs are finite; a program needn't handle non-finite values.
Results may differ from the reference program's by a relative error of at most 0.0085.
Values may be sent and summed in bfloat16 or wider, within the bound.
No kernel may reach another device: no remote copies, remote signals or barrier semaphores. Data moves between devices by JAX's collectives and lax.ppermute only.
A program may use at most 128 MiB of HBM per device.

```python
import jax
import jax.numpy as jnp

D = 8192
FF = 26624
TOKENS = 128


def block_scale(own_key, dims, cuts, low, top_value):
    level = 1.0
    for axis_at, parts in cuts:
        steps = jax.random.uniform(jax.random.fold_in(jax.random.fold_in(own_key, 6), axis_at), (parts,), jnp.float32, low / len(cuts), top_value / len(cuts))
        level = level * jnp.repeat(jnp.exp(steps), dims[axis_at] // parts).reshape((-1,) + (1,) * (len(dims) - 1 - axis_at))
    return level


def scatter_about(key, shape, scale, limit, pieces=(), held_as=jnp.bfloat16):
    gain = block_scale(key, shape, pieces, -0.22, 0.18) if pieces else 1.0
    drawn = jax.random.normal(key, shape, jnp.float32) * scale * gain
    return jnp.minimum(jnp.maximum(drawn, -limit), limit).astype(held_as)


def setup_inputs(seed: int = 0) -> dict:
    arg_keys = jax.random.split(jax.random.key(seed), 7)
    tokens = scatter_about(arg_keys[0], (TOKENS, D), 1.0, 6.0, ((0, 8), (1, 16)))
    gate_weight = scatter_about(arg_keys[1], (D, FF), D ** -0.5, 0.0625, ((0, 16), (1, 8)))
    up_weight = scatter_about(arg_keys[2], (D, FF), D ** -0.5, 0.0625, ((0, 16), (1, 8)))
    down_weight = scatter_about(arg_keys[3], (FF, D), FF ** -0.5, 0.0390625, ((0, 8), (1, 16)))
    gate_tangent = scatter_about(arg_keys[4], (D, FF), D ** -0.5, 0.0625, ((0, 16), (1, 8)))
    up_tangent = scatter_about(arg_keys[5], (D, FF), D ** -0.5, 0.0625, ((0, 16), (1, 8)))
    return {"tokens": tokens, "gate_weight": gate_weight, "up_weight": up_weight, "down_weight": down_weight, "gate_tangent": gate_tangent, "up_tangent": up_tangent}


def matmul(left, right):
    return jnp.dot(left, right, preferred_element_type=jnp.float32)


def silu_terms(gate_sum):
    sigmoid_val = jax.nn.sigmoid(gate_sum)
    return gate_sum * sigmoid_val, sigmoid_val * (1.0 + gate_sum * (1.0 - sigmoid_val))


def reference(tokens, gate_weight, up_weight, down_weight, gate_tangent, up_tangent):
    gate_sum = matmul(tokens, gate_weight)
    up_sum = matmul(tokens, up_weight)
    gate_dir = matmul(tokens, gate_tangent)
    up_dir = matmul(tokens, up_tangent)
    activated, slopes = silu_terms(gate_sum)
    hidden_dir = (slopes * gate_dir * up_sum + activated * up_dir).astype(jnp.bfloat16)
    out_scale = float(TOKENS) ** -0.5
    output_dir = (matmul(hidden_dir, down_weight) * out_scale).astype(jnp.bfloat16)
    back_sum = matmul(output_dir, down_weight.T)
    gate_cot = (back_sum * up_sum * slopes).astype(jnp.bfloat16)
    up_cot = (back_sum * activated).astype(jnp.bfloat16)
    gate_product = matmul(tokens.T, gate_cot).astype(jnp.bfloat16)
    up_product = matmul(tokens.T, up_cot).astype(jnp.bfloat16)
    return gate_product, up_product
```

```python
import jax
import jax.numpy as jnp
from jax import lax
from jax.sharding import PartitionSpec as P

BF = jnp.bfloat16
F32 = jnp.float32
RC = ("row", "col")


def device(z, k, y, x):
    return ((z % 4) * 2 + k) * 16 + (y % 4) * 4 + (x % 4)


def pairs(move):
    return [
        (device(z, k, y, x), device(*move(z, k, y, x)))
        for z in range(4)
        for k in range(2)
        for y in range(4)
        for x in range(4)
    ]


def near(i):
    return i ^ 1


def far(i):
    return i + 1 if i % 2 else i - 1


def along_first(move):
    return pairs(lambda z, k, y, x: (z, k, y, move(x)) if k == 0 else (z, k, move(y), x))


def along_second(move):
    return pairs(lambda z, k, y, x: (z, k, move(y), x) if k == 0 else (z, k, y, move(x)))


CORE = pairs(lambda z, k, y, x: (z, 1 - k, y, x))


def z_shift(d):
    return pairs(lambda z, k, y, x: (z + d, k, y, x))


def first_shift(d):
    return along_first(lambda i: i + d)


def second_shift(d):
    return along_second(lambda i: i + d)


def send(value, to):
    return lax.ppermute(value, RC, to)


def matmul(left, right):
    return jnp.dot(left, right, preferred_element_type=F32)


def against_rows(left, right):
    return lax.dot_general(left, right, (((1,), (1,)), ((), ())), preferred_element_type=F32)


def transposed(left, right):
    return lax.dot_general(left, right, (((0,), (0,)), ((), ())), preferred_element_type=F32)


def gather_tokens(tokens, z, k):
    chip = jnp.concatenate([tokens, send(tokens, CORE)])
    return jnp.concatenate([chip] + [send(chip, z_shift(d)) for d in (1, 2, 3)])


def row_order(first, second, z, k, x, y):
    first = jnp.repeat(first, 32)
    second = jnp.tile(jnp.repeat(second, 8), 4)
    high = (x + jnp.where(k == 0, first, second)) % 4
    low = (y + jnp.where(k == 0, second, first)) % 4
    token = (high * 4 + low) * 8 + jnp.tile(jnp.arange(8), 16)
    return ((z - token // 32) % 4) * 32 + ((token // 16 % 2) ^ k) * 16 + token % 16


def halve(left, right, tokens, to_half, to_quarter):
    full = jnp.stack([matmul(tokens, left), matmul(tokens, right)])
    got = send(full[:, 64:].astype(BF), to_half)
    half = full[:, :64] + got
    got = send(half[:, 32:].astype(BF), to_quarter)
    return half[:, :32] + got


def scatter_second(quarter):
    got = [send(quarter[:, 8 * e : 8 * e + 8].astype(BF), second_shift(e)) for e in (1, 2, 3)]
    return quarter[:, :8] + got[0] + got[1] + got[2]


def scatter_first(full):
    got = [send(full[:, 32 * d : 32 * d + 32].astype(BF), first_shift(d)) for d in (1, 2, 3)]
    return full[:, :32] + got[0] + got[1] + got[2]


def gather_second(own):
    return jnp.concatenate([own] + [send(own, second_shift(-e)) for e in (1, 2, 3)], axis=1)


def gather_first(own):
    return jnp.concatenate([own] + [send(own, first_shift(-d)) for d in (1, 2, 3)], axis=1)


def swap_axes(value):
    return value.reshape(4, 4, 8, -1).swapaxes(0, 1).reshape(value.shape)


def sum_rows(part, k):
    part = jnp.where(k == 0, part, swap_axes(part))
    mine = jnp.where(k == 0, part[:64], part[64:])
    other = jnp.where(k == 0, part[64:], part[:64])
    mine = mine + send(other, CORE)
    rounded = mine.astype(BF)
    got = [send(rounded, z_shift(d)) for d in (1, 2, 3)]
    return mine + got[0] + got[1] + got[2]


def join_halves(half, k):
    other = send(half, CORE)
    full = jnp.where(k == 0, jnp.concatenate([half, other]), jnp.concatenate([other, half]))
    return jnp.where(k == 0, full, swap_axes(full))


def body(tokens, gate_weight, up_weight, down_weight, gate_tangent, up_tangent):
    row, col = lax.axis_index("row"), lax.axis_index("col")
    z, k, y, x = row // 2, row % 2, col // 4, col % 4
    out_scale = 128.0 ** (-0.5)
    gathered = gather_tokens(tokens, z, k)
    step = 1 - 2 * (jnp.where(k == 0, x, y) % 2)
    straight = jnp.arange(4)
    orders = jnp.concatenate(
        [
            row_order(jnp.stack([0 * step, -step, step, 2 + 0 * step]), straight, z, k, x, y),
            row_order(jnp.stack([0 * step, step, -step, 2 + 0 * step]), straight, z, k, x, y),
            row_order(straight, straight, z, k, x, y),
        ]
    )
    picked = (orders[:, None] == jnp.arange(128)[None, :]).astype(BF)
    placed = matmul(picked, gathered).astype(BF)
    tokens_a, tokens_b, local = placed[:128], placed[128:256], placed[256:]

    sums = halve(gate_weight, up_weight, tokens_a, along_first(near), along_first(far))
    dirs = halve(gate_tangent, up_tangent, tokens_b, along_first(far), along_first(near))
    gate_sum, up_sum, gate_dir, up_dir = scatter_second(jnp.concatenate([sums, dirs]))
    sigmoid = jax.nn.sigmoid(gate_sum)
    activated = gate_sum * sigmoid
    up_slopes = up_sum * (sigmoid * (1.0 + gate_sum * (1.0 - sigmoid)))
    hidden = (up_slopes * gate_dir + activated * up_dir).astype(BF)

    hidden = gather_first(gather_second(hidden[None]))[0]
    half = sum_rows(matmul(hidden, down_weight), k)
    output_dir = join_halves((half * out_scale).astype(BF), k)
    back = scatter_second(scatter_first(against_rows(output_dir, down_weight)[None]))[0]
    cots = jnp.stack([back * up_slopes, back * activated]).astype(BF)
    gate_cot, up_cot = gather_first(gather_second(cots))
    return transposed(local, gate_cot).astype(BF), transposed(local, up_cot).astype(BF)


def solution(mesh):
    placed = (
        P("row", "col"),
        P("col", "row"),
        P("col", "row"),
        P("row", "col"),
        P("col", "row"),
        P("col", "row"),
    )
    return jax.shard_map(
        body,
        mesh=mesh,
        in_specs=placed,
        out_specs=(P("col", "row"), P("col", "row")),
        check_vma=False,
    )
```

```python
import jax
import jax.numpy as jnp
from jax import lax
from jax.sharding import PartitionSpec as P

BF = jnp.bfloat16
F32 = jnp.float32
RC = ("row", "col")


def device(z, k, y, x):
    return ((z % 4) * 2 + k) * 16 + (y % 4) * 4 + (x % 4)


def pairs(move):
    return [
        (device(z, k, y, x), device(*move(z, k, y, x)))
        for z in range(4)
        for k in range(2)
        for y in range(4)
        for x in range(4)
    ]


def along_first(move):
    return pairs(lambda z, k, y, x: (z, k, y, move(x)) if k == 0 else (z, k, move(y), x))


def along_second(move):
    return pairs(lambda z, k, y, x: (z, k, move(y), x) if k == 0 else (z, k, y, move(x)))


CORE = pairs(lambda z, k, y, x: (z, 1 - k, y, x))


def z_shift(d):
    return pairs(lambda z, k, y, x: (z + d, k, y, x))


def first_shift(d):
    return along_first(lambda i: i + d)


def second_shift(d):
    return along_second(lambda i: i + d)


def send(value, to):
    return lax.ppermute(value, RC, to)


def matmul(left, right):
    return jnp.dot(left, right, preferred_element_type=F32)


def against_rows(left, right):
    return lax.dot_general(left, right, (((1,), (1,)), ((), ())), preferred_element_type=F32)


def transposed(left, right):
    return lax.dot_general(left, right, (((0,), (0,)), ((), ())), preferred_element_type=F32)


def gather_tokens(tokens, z, k):
    chip = jnp.concatenate([tokens, send(tokens, CORE)])
    return jnp.concatenate([chip] + [send(chip, z_shift(d)) for d in (1, 2, 3)])


def row_order(z, k, x, y):
    first = jnp.repeat(jnp.arange(4), 32)
    second = jnp.tile(jnp.repeat(jnp.arange(4), 8), 4)
    high = (x + jnp.where(k == 0, first, second)) % 4
    low = (y + jnp.where(k == 0, second, first)) % 4
    token = (high * 4 + low) * 8 + jnp.tile(jnp.arange(8), 16)
    return ((z - token // 32) % 4) * 32 + ((token // 16 % 2) ^ k) * 16 + token % 16


def scatter_second(quarter):
    got = [send(quarter[:, 8 * e : 8 * e + 8].astype(BF), second_shift(e)) for e in (2, 1, 3)]
    return quarter[:, :8] + got[0] + got[1] + got[2]


def scatter_first(full):
    got = [send(full[:, 32 * d : 32 * d + 32].astype(BF), first_shift(d)) for d in (2, 1, 3)]
    return full[:, :32] + got[0] + got[1] + got[2]


def sum_second(part):
    rounded = part.astype(BF)
    for e in (2, 1, 3):
        part = part + jnp.roll(send(rounded, second_shift(e)), -8 * e, axis=0)
    return part


def gather_second(own):
    got = {e: send(own, second_shift(-e)) for e in (2, 1, 3)}
    return jnp.concatenate([own, got[1], got[2], got[3]], axis=1)


def gather_first(own):
    got = {d: send(own, first_shift(-d)) for d in (2, 1, 3)}
    return jnp.concatenate([own, got[1], got[2], got[3]], axis=1)


def swap_axes(value):
    return value.reshape(4, 4, 8, -1).swapaxes(0, 1).reshape(value.shape)


def sum_rows(part, k):
    part = jnp.where(k == 0, part, swap_axes(part))
    mine = jnp.where(k == 0, part[:64], part[64:])
    other = jnp.where(k == 0, part[64:], part[:64])
    mine = mine + send(other, CORE)
    rounded = mine.astype(BF)
    got = [send(rounded, z_shift(d)) for d in (1, 2, 3)]
    return mine + got[0] + got[1] + got[2]


def join_halves(half, k):
    other = send(half, CORE)
    full = jnp.where(k == 0, jnp.concatenate([half, other]), jnp.concatenate([other, half]))
    return jnp.where(k == 0, full, swap_axes(full))


def body(tokens, gate_weight, up_weight, down_weight, gate_tangent, up_tangent):
    row, col = lax.axis_index("row"), lax.axis_index("col")
    z, k, y, x = row // 2, row % 2, col // 4, col % 4
    out_scale = 128.0 ** (-0.5)
    gathered = gather_tokens(tokens, z, k)
    order = row_order(z, k, x, y)
    picked = (order[:, None] == jnp.arange(128)[None, :]).astype(BF)
    local = matmul(picked, gathered).astype(BF)

    def hidden_sums(left, right):
        full = jnp.stack([matmul(local, left), matmul(local, right)])
        return scatter_second(scatter_first(full))

    gate_sum, up_sum = hidden_sums(gate_weight, up_weight)
    gate_dir, up_dir = hidden_sums(gate_tangent, up_tangent)
    sigmoid = jax.nn.sigmoid(gate_sum)
    activated = gate_sum * sigmoid
    up_slopes = up_sum * (sigmoid * (1.0 + gate_sum * (1.0 - sigmoid)))
    hidden = (up_slopes * gate_dir + activated * up_dir).astype(BF)

    hidden, activated, up_slopes = gather_second(
        jnp.stack([hidden, activated.astype(BF), up_slopes.astype(BF)])
    )
    hidden = gather_first(hidden[None])[0]
    half = sum_rows(matmul(hidden, down_weight), k)
    output_dir = join_halves((half * out_scale).astype(BF), k)
    back = sum_second(scatter_first(against_rows(output_dir, down_weight)[None])[0])
    gate_cot = gather_first((back * up_slopes).astype(BF)[None])[0]
    up_cot = gather_first((back * activated).astype(BF)[None])[0]
    return transposed(local, gate_cot).astype(BF), transposed(local, up_cot).astype(BF)


def solution(mesh):
    placed = (
        P("row", "col"),
        P("col", "row"),
        P("col", "row"),
        P("row", "col"),
        P("col", "row"),
        P("col", "row"),
    )
    return jax.shard_map(
        body,
        mesh=mesh,
        in_specs=placed,
        out_specs=(P("col", "row"), P("col", "row")),
        check_vma=False,
    )
```

```python
import jax
import jax.numpy as jnp
from jax import lax
from jax.experimental import pallas as pl
from jax.experimental.pallas import tpu as pltpu
from jax.sharding import PartitionSpec as P

BF = jnp.bfloat16
F32 = jnp.float32
RC = ("row", "col")


def device(z, k, y, x):
    return ((z % 4) * 2 + k) * 16 + (y % 4) * 4 + (x % 4)


def pairs(move):
    return [
        (device(z, k, y, x), device(*move(z, k, y, x)))
        for z in range(4)
        for k in range(2)
        for y in range(4)
        for x in range(4)
    ]


def near(i):
    return i ^ 1


def far(i):
    return i + 1 if i % 2 else i - 1


def along_first(move):
    return pairs(lambda z, k, y, x: (z, k, y, move(x)) if k == 0 else (z, k, move(y), x))


def along_second(move):
    return pairs(lambda z, k, y, x: (z, k, move(y), x) if k == 0 else (z, k, y, move(x)))


CORE = pairs(lambda z, k, y, x: (z, 1 - k, y, x))


def z_shift(d):
    return pairs(lambda z, k, y, x: (z + d, k, y, x))


def first_shift(d):
    return along_first(lambda i: i + d)


def second_shift(d):
    return along_second(lambda i: i + d)


def send(value, to):
    return lax.ppermute(value, RC, to)


def matmul(left, right):
    return jnp.dot(left, right, preferred_element_type=F32)


def against_rows(left, right):
    return lax.dot_general(left, right, (((1,), (1,)), ((), ())), preferred_element_type=F32)


def transposed(left, right):
    return lax.dot_general(left, right, (((0,), (0,)), ((), ())), preferred_element_type=F32)


def gather_tokens(tokens, ready):
    got = {d: send(tokens, z_shift(d)) for d in (2, 1, 3)}
    own = jnp.concatenate([tokens, got[1], got[2], got[3]])
    own = after(own, ready)
    return own, send(own, CORE)


def order_matrix(offsets, z, k, x, y):
    local = lax.broadcasted_iota(jnp.int32, (128, 128), 0)
    column = lax.broadcasted_iota(jnp.int32, (128, 128), 1)
    block, second = local // 32, local // 8 % 4
    first = jnp.where(
        block == 1, offsets[1], jnp.where(block == 2, offsets[2], jnp.where(block == 3, offsets[3], offsets[0]))
    )
    high = (x + jnp.where(k == 0, first, second)) & 3
    low = (y + jnp.where(k == 0, second, first)) & 3
    token = (high * 4 + low) * 8 + local % 8
    place = ((token // 16 & 1) ^ k) * 64 + ((z - token // 32) & 3) * 16 + token % 16
    return (place == column).astype(BF)


def into_vmem(array):
    rows, width = array.shape
    cut = 4

    def kernel(source, target, sems):
        copies = [
            pltpu.make_async_copy(
                source.at[pl.ds(i * rows // cut, rows // cut)],
                target.at[pl.ds(i * rows // cut, rows // cut)],
                sems.at[i],
            )
            for i in range(cut)
        ]
        for copy in copies:
            copy.start()
        for copy in copies:
            copy.wait()

    return pl.pallas_call(
        kernel,
        out_shape=jax.ShapeDtypeStruct(array.shape, array.dtype),
        in_specs=[pl.BlockSpec(memory_space=pltpu.HBM)],
        out_specs=pl.BlockSpec(memory_space=pltpu.VMEM),
        scratch_shapes=[pltpu.SemaphoreType.DMA((cut,))],
        compiler_params=pltpu.CompilerParams(vmem_limit_bytes=32 << 20),
        cost_estimate=pl.CostEstimate(
            flops=0, bytes_accessed=array.size * 2, transcendentals=0
        ),
        name="into_vmem",
    )(array)


def product(local, cot):
    features, width = local.shape[1], cot.shape[1]
    step = 256
    count = width // step

    def kernel(local_ref, cot_ref, out, held, sems):
        left = local_ref[...].T
        copies = []
        for i in range(count):
            at = pl.ds(i * step, step)
            held[:, at] = matmul(left, cot_ref[:, at]).astype(BF)
            copies.append(pltpu.make_async_copy(held.at[:, at], out.at[:, at], sems.at[i]))
            copies[-1].start()
        for copy in copies:
            copy.wait()

    return pl.pallas_call(
        kernel,
        out_shape=jax.ShapeDtypeStruct((features, width), BF),
        in_specs=[pl.BlockSpec(memory_space=pltpu.VMEM)] * 2,
        out_specs=pl.BlockSpec(memory_space=pltpu.HBM),
        scratch_shapes=[
            pltpu.VMEM((features, width), BF),
            pltpu.SemaphoreType.DMA((count,)),
        ],
        compiler_params=pltpu.CompilerParams(vmem_limit_bytes=32 << 20),
        name="product",
    )(local, cot)


def after(value, other):
    return lax.optimization_barrier((value, other))[0]


def halve(tokens, weight, to_half, to_quarter):
    full = matmul(tokens, weight)
    away = full[64:].astype(BF)
    half = full[:64] + send(away, to_half)
    return half[:32] + send(half[32:].astype(BF), to_quarter), away


def scatter_second(quarter):
    got = [send(quarter[:, 8 * e : 8 * e + 8].astype(BF), second_shift(e)) for e in (2, 1, 3)]
    return quarter[:, :8] + got[0] + got[1] + got[2]


def scatter_first(full):
    got = [send(full[:, 32 * d : 32 * d + 32].astype(BF), first_shift(d)) for d in (2, 1, 3)]
    return full[:, :32] + got[0] + got[1] + got[2]


def sum_second(part):
    rounded = part.astype(BF)
    for e in (2, 1, 3):
        part = part + jnp.roll(send(rounded, second_shift(e)), -8 * e, axis=0)
    return part


def gather_second(own):
    got = {e: send(own, second_shift(-e)) for e in (2, 1, 3)}
    return jnp.concatenate([own, got[1], got[2], got[3]], axis=1)


def gather_first(own):
    got = {d: send(own, first_shift(-d)) for d in (2, 1, 3)}
    return jnp.concatenate([own, got[1], got[2], got[3]], axis=1)


def swap_axes(value):
    return value.reshape(4, 4, 8, -1).swapaxes(0, 1).reshape(value.shape)


def sum_rows(part, factors, k):
    part = jnp.where(k == 0, part, swap_axes(part))
    mine = jnp.where(k == 0, part[:64], part[64:])
    other = jnp.where(k == 0, part[64:], part[:64])
    mine = mine + send(other, CORE)
    rounded = mine.astype(BF)
    got = [send(rounded, z_shift(d)) for d in (1, 2, 3)]
    factors = gather_second(after(factors, rounded))
    return mine + got[0] + got[1] + got[2], factors[0], factors[1]


def join_halves(half, k):
    other = send(half, CORE)
    full = jnp.where(k == 0, jnp.concatenate([half, other]), jnp.concatenate([other, half]))
    return jnp.where(k == 0, full, swap_axes(full))


def body(tokens, gate_weight, up_weight, down_weight, gate_tangent, up_tangent):
    row, col = lax.axis_index("row"), lax.axis_index("col")
    z, k, y, x = row // 2, row % 2, col // 4, col % 4
    out_scale = 128.0 ** (-0.5)
    gate_weight = into_vmem(gate_weight)
    own, other = gather_tokens(tokens, gate_weight)
    turn = 1 - 2 * (jnp.where(k == 0, x, y) & 1)

    def ordered(*offsets):
        picked = order_matrix(offsets, z, k, x, y)
        return (matmul(picked[:, :64], own) + matmul(picked[:, 64:], other)).astype(BF)

    ahead, behind = ordered(0, -turn, turn, 2), ordered(0, turn, -turn, 2)
    local = ordered(0, 1, 2, 3)
    near_far = along_first(near), along_first(far)
    far_near = along_first(far), along_first(near)
    gate_sum, sent = halve(ahead, gate_weight, *near_far)
    up_sum, sent = halve(after(behind, sent), up_weight, *far_near)
    gate_dir, sent = halve(after(ahead, sent), gate_tangent, *near_far)
    up_dir, sent = halve(after(behind, sent), up_tangent, *far_near)
    gate_sum, up_sum, gate_dir, up_dir = scatter_second(
        jnp.stack([gate_sum, up_sum, gate_dir, up_dir])
    )
    sigmoid = jax.nn.sigmoid(gate_sum)
    activated = gate_sum * sigmoid
    up_slopes = up_sum * (sigmoid * (1.0 + gate_sum * (1.0 - sigmoid)))
    hidden = (up_slopes * gate_dir + activated * up_dir).astype(BF)

    hidden = gather_first(gather_second(hidden[None]))[0]
    half, up_slopes, activated = sum_rows(
        matmul(hidden, down_weight), jnp.stack([up_slopes, activated]).astype(BF), k
    )
    output_dir = join_halves((half * out_scale).astype(BF), k)
    back = sum_second(scatter_first(against_rows(output_dir, down_weight)[None])[0])
    gate_cot = gather_first((back * up_slopes).astype(BF)[None])[0]
    up_cot = gather_first((back * activated).astype(BF)[None])[0]
    return product(local, gate_cot), product(local, up_cot)


def solution(mesh):
    placed = (
        P("row", "col"),
        P("col", "row"),
        P("col", "row"),
        P("row", "col"),
        P("col", "row"),
        P("col", "row"),
    )
    return jax.shard_map(
        body,
        mesh=mesh,
        in_specs=placed,
        out_specs=(P("col", "row"), P("col", "row")),
        check_vma=False,
    )
```

```python
import jax
import jax.numpy as jnp
from jax import lax
from jax.experimental import pallas as pl
from jax.experimental.pallas import tpu as pltpu
from jax.sharding import PartitionSpec as P

BF = jnp.bfloat16
F32 = jnp.float32
RC = ("row", "col")


def device(z, k, y, x):
    return ((z % 4) * 2 + k) * 16 + (y % 4) * 4 + (x % 4)


def pairs(move):
    return [
        (device(z, k, y, x), device(*move(z, k, y, x)))
        for z in range(4)
        for k in range(2)
        for y in range(4)
        for x in range(4)
    ]


def near(i):
    return i ^ 1


def far(i):
    return i + 1 if i % 2 else i - 1


def along_first(move):
    return pairs(lambda z, k, y, x: (z, k, y, move(x)) if k == 0 else (z, k, move(y), x))


def along_second(move):
    return pairs(lambda z, k, y, x: (z, k, move(y), x) if k == 0 else (z, k, y, move(x)))


CORE = pairs(lambda z, k, y, x: (z, 1 - k, y, x))


def z_shift(d):
    return pairs(lambda z, k, y, x: (z + d, k, y, x))


def first_shift(d):
    return along_first(lambda i: i + d)


def second_shift(d):
    return along_second(lambda i: i + d)


def send(value, to):
    return lax.ppermute(value, RC, to)


def matmul(left, right):
    return jnp.dot(left, right, preferred_element_type=F32)


def against_rows(left, right):
    return lax.dot_general(left, right, (((1,), (1,)), ((), ())), preferred_element_type=F32)


def transposed(left, right):
    return lax.dot_general(left, right, (((0,), (0,)), ((), ())), preferred_element_type=F32)


def gather_tokens(tokens, ready):
    got = {d: send(tokens, z_shift(d)) for d in (2, 1, 3)}
    own = jnp.concatenate([tokens, got[1], got[2], got[3]])
    own = after(own, ready)
    return own, send(own, CORE)


def order_matrix(offsets, z, k, x, y):
    local = lax.broadcasted_iota(jnp.int32, (128, 128), 0)
    column = lax.broadcasted_iota(jnp.int32, (128, 128), 1)
    block, second = local // 32, local // 8 % 4
    first = jnp.where(
        block == 1, offsets[1], jnp.where(block == 2, offsets[2], jnp.where(block == 3, offsets[3], offsets[0]))
    )
    high = (x + jnp.where(k == 0, first, second)) & 3
    low = (y + jnp.where(k == 0, second, first)) & 3
    token = (high * 4 + low) * 8 + local % 8
    place = ((token // 16 & 1) ^ k) * 64 + ((z - token // 32) & 3) * 16 + token % 16
    return (place == column).astype(BF)


def into_vmem(array):
    rows, width = array.shape
    cut = 4

    def kernel(source, target, sems):
        copies = [
            pltpu.make_async_copy(
                source.at[pl.ds(i * rows // cut, rows // cut)],
                target.at[pl.ds(i * rows // cut, rows // cut)],
                sems.at[i],
            )
            for i in range(cut)
        ]
        for copy in copies:
            copy.start()
        for copy in copies:
            copy.wait()

    return pl.pallas_call(
        kernel,
        out_shape=jax.ShapeDtypeStruct(array.shape, array.dtype),
        in_specs=[pl.BlockSpec(memory_space=pltpu.HBM)],
        out_specs=pl.BlockSpec(memory_space=pltpu.VMEM),
        scratch_shapes=[pltpu.SemaphoreType.DMA((cut,))],
        compiler_params=pltpu.CompilerParams(vmem_limit_bytes=32 << 20),
        cost_estimate=pl.CostEstimate(
            flops=0, bytes_accessed=array.size * 2, transcendentals=0
        ),
        name="into_vmem",
    )(array)


def product(local, cot):
    features, width = local.shape[1], cot.shape[1]
    step = 256
    count = width // step

    def kernel(local_ref, cot_ref, out, held, sems):
        left = local_ref[...].T
        copies = []
        for i in range(count):
            at = pl.ds(i * step, step)
            held[:, at] = matmul(left, cot_ref[:, at]).astype(BF)
            copies.append(pltpu.make_async_copy(held.at[:, at], out.at[:, at], sems.at[i]))
            copies[-1].start()
        for copy in copies:
            copy.wait()

    return pl.pallas_call(
        kernel,
        out_shape=jax.ShapeDtypeStruct((features, width), BF),
        in_specs=[pl.BlockSpec(memory_space=pltpu.VMEM)] * 2,
        out_specs=pl.BlockSpec(memory_space=pltpu.HBM),
        scratch_shapes=[
            pltpu.VMEM((features, width), BF),
            pltpu.SemaphoreType.DMA((count,)),
        ],
        compiler_params=pltpu.CompilerParams(vmem_limit_bytes=32 << 20),
        name="product",
    )(local, cot)


def after(value, other):
    return lax.optimization_barrier((value, other))[0]


def halve(tokens, weight, to_half, to_quarter):
    full = matmul(tokens, weight)
    away = full[64:].astype(BF)
    half = full[:64] + send(away, to_half)
    return half[:32] + send(half[32:].astype(BF), to_quarter), away


def scatter_second(quarter):
    got = [send(quarter[:, 8 * e : 8 * e + 8].astype(BF), second_shift(e)) for e in (2, 1, 3)]
    return quarter[:, :8] + got[0] + got[1] + got[2]


def scatter_first(full):
    got = [send(full[:, 32 * d : 32 * d + 32].astype(BF), first_shift(d)) for d in (2, 1, 3)]
    return full[:, :32] + got[0] + got[1] + got[2]


def sum_second(part):
    rounded = part.astype(BF)
    for e in (2, 1, 3):
        part = part + jnp.roll(send(rounded, second_shift(e)), -8 * e, axis=0)
    return part


def gather_second(own):
    got = {e: send(own, second_shift(-e)) for e in (2, 1, 3)}
    return jnp.concatenate([own, got[1], got[2], got[3]], axis=1)


def gather_second_pairs(own, next_, even):
    both = send(jnp.concatenate([own, next_], axis=1), along_second(far))
    before, across = both[:, :8], both[:, 8:]
    return jnp.concatenate(
        [own, jnp.where(even, next_, before), across, jnp.where(even, before, next_)], axis=1
    )


def gather_first(own):
    got = {d: send(own, first_shift(-d)) for d in (2, 1, 3)}
    return jnp.concatenate([own, got[1], got[2], got[3]], axis=1)


def swap_axes(value):
    return value.reshape(4, 4, 8, -1).swapaxes(0, 1).reshape(value.shape)


def sum_rows(part, factors, next_, k, even):
    part = jnp.where(k == 0, part, swap_axes(part))
    mine = jnp.where(k == 0, part[:64], part[64:])
    other = jnp.where(k == 0, part[64:], part[:64])
    mine = mine + send(other, CORE)
    rounded = mine.astype(BF)
    got = [send(rounded, z_shift(d)) for d in (1, 2, 3)]
    factors = gather_second_pairs(factors, after(next_, mine), even)
    return mine + got[0] + got[1] + got[2], factors[0], factors[1]


def join_halves(half, k):
    other = send(half, CORE)
    full = jnp.where(k == 0, jnp.concatenate([half, other]), jnp.concatenate([other, half]))
    return jnp.where(k == 0, full, swap_axes(full))


def body(tokens, gate_weight, up_weight, down_weight, gate_tangent, up_tangent):
    row, col = lax.axis_index("row"), lax.axis_index("col")
    z, k, y, x = row // 2, row % 2, col // 4, col % 4
    even = jnp.where(k == 0, y, x) & 1 == 0
    out_scale = 128.0 ** (-0.5)
    gate_weight = into_vmem(gate_weight)
    own, other = gather_tokens(tokens, gate_weight)
    turn = 1 - 2 * (jnp.where(k == 0, x, y) & 1)

    def ordered(*offsets):
        picked = order_matrix(offsets, z, k, x, y)
        return (matmul(picked[:, :64], own) + matmul(picked[:, 64:], other)).astype(BF)

    ahead, behind = ordered(0, -turn, turn, 2), ordered(0, turn, -turn, 2)
    local = ordered(0, 1, 2, 3)
    near_far = along_first(near), along_first(far)
    far_near = along_first(far), along_first(near)
    gate_sum, sent = halve(ahead, gate_weight, *near_far)
    up_sum, sent = halve(after(behind, sent), up_weight, *far_near)
    gate_dir, sent = halve(after(ahead, sent), gate_tangent, *near_far)
    up_dir, sent = halve(after(behind, sent), up_tangent, *far_near)
    gate_sum, up_sum, gate_dir, up_dir = scatter_second(
        jnp.stack([gate_sum, up_sum, gate_dir, up_dir])
    )
    sigmoid = jax.nn.sigmoid(gate_sum)
    activated = gate_sum * sigmoid
    up_slopes = up_sum * (sigmoid * (1.0 + gate_sum * (1.0 - sigmoid)))
    hidden = (up_slopes * gate_dir + activated * up_dir).astype(BF)

    factors = jnp.stack([up_slopes, activated]).astype(BF)
    hidden = gather_second(hidden[None])
    next_ = send(after(factors, hidden), along_second(near))
    hidden = after(gather_first(hidden)[0], next_)
    half, up_slopes, activated = sum_rows(matmul(hidden, down_weight), factors, next_, k, even)
    output_dir = join_halves((half * out_scale).astype(BF), k)
    back = sum_second(scatter_first(against_rows(output_dir, down_weight)[None])[0])
    gate_cot = gather_first((back * up_slopes).astype(BF)[None])[0]
    up_cot = gather_first((back * activated).astype(BF)[None])[0]
    return product(local, gate_cot), product(local, up_cot)


def solution(mesh):
    placed = (
        P("row", "col"),
        P("col", "row"),
        P("col", "row"),
        P("row", "col"),
        P("col", "row"),
        P("col", "row"),
    )
    return jax.shard_map(
        body,
        mesh=mesh,
        in_specs=placed,
        out_specs=(P("col", "row"), P("col", "row")),
        check_vma=False,
    )
```

```python
import jax
import jax.numpy as jnp
from jax import lax
from jax.experimental import pallas as pl
from jax.experimental.pallas import tpu as pltpu
from jax.sharding import PartitionSpec as P

BF = jnp.bfloat16
F32 = jnp.float32
RC = ("row", "col")


def device(z, k, y, x):
    return ((z % 4) * 2 + k) * 16 + (y % 4) * 4 + (x % 4)


def pairs(move):
    return [
        (device(z, k, y, x), device(*move(z, k, y, x)))
        for z in range(4)
        for k in range(2)
        for y in range(4)
        for x in range(4)
    ]


def near(i):
    return i ^ 1


def far(i):
    return i + 1 if i % 2 else i - 1


def along_first(move):
    return pairs(lambda z, k, y, x: (z, k, y, move(x)) if k == 0 else (z, k, move(y), x))


def along_second(move):
    return pairs(lambda z, k, y, x: (z, k, move(y), x) if k == 0 else (z, k, y, move(x)))


CORE = pairs(lambda z, k, y, x: (z, 1 - k, y, x))


def z_shift(d):
    return pairs(lambda z, k, y, x: (z + d, k, y, x))


def first_shift(d):
    return along_first(lambda i: i + d)


def second_shift(d):
    return along_second(lambda i: i + d)


def send(value, to):
    return lax.ppermute(value, RC, to)


def matmul(left, right):
    return jnp.dot(left, right, preferred_element_type=F32)


def against_rows(left, right):
    return lax.dot_general(left, right, (((1,), (1,)), ((), ())), preferred_element_type=F32)


def transposed(left, right):
    return lax.dot_general(left, right, (((0,), (0,)), ((), ())), preferred_element_type=F32)


def gather_tokens(tokens, ready):
    got = {d: send(tokens, z_shift(d)) for d in (2, 1, 3)}
    own = jnp.concatenate([tokens, got[1], got[2], got[3]])
    own = after(own, ready)
    return own, send(own, CORE)


def order_matrix(offsets, z, k, x, y):
    local = lax.broadcasted_iota(jnp.int32, (128, 128), 0)
    column = lax.broadcasted_iota(jnp.int32, (128, 128), 1)
    block, second = local // 32, local // 8 % 4
    first = jnp.where(
        block == 1, offsets[1], jnp.where(block == 2, offsets[2], jnp.where(block == 3, offsets[3], offsets[0]))
    )
    high = (x + jnp.where(k == 0, first, second)) & 3
    low = (y + jnp.where(k == 0, second, first)) & 3
    token = (high * 4 + low) * 8 + local % 8
    place = ((token // 16 & 1) ^ k) * 64 + ((z - token // 32) & 3) * 16 + token % 16
    return (place == column).astype(BF)


def into_vmem(array):
    rows, width = array.shape
    cut = 4

    def kernel(source, target, sems):
        copies = [
            pltpu.make_async_copy(
                source.at[pl.ds(i * rows // cut, rows // cut)],
                target.at[pl.ds(i * rows // cut, rows // cut)],
                sems.at[i],
            )
            for i in range(cut)
        ]
        for copy in copies:
            copy.start()
        for copy in copies:
            copy.wait()

    return pl.pallas_call(
        kernel,
        out_shape=jax.ShapeDtypeStruct(array.shape, array.dtype),
        in_specs=[pl.BlockSpec(memory_space=pltpu.HBM)],
        out_specs=pl.BlockSpec(memory_space=pltpu.VMEM),
        scratch_shapes=[pltpu.SemaphoreType.DMA((cut,))],
        compiler_params=pltpu.CompilerParams(vmem_limit_bytes=32 << 20),
        cost_estimate=pl.CostEstimate(
            flops=0, bytes_accessed=array.size * 2, transcendentals=0
        ),
        name="into_vmem",
    )(array)


def product(local, cot):
    features, width = local.shape[1], cot.shape[1]
    step = 256
    count = width // step

    def kernel(local_ref, cot_ref, out, held, sems):
        left = local_ref[...].T
        copies = []
        for i in range(count):
            at = pl.ds(i * step, step)
            held[:, at] = matmul(left, cot_ref[:, at]).astype(BF)
            copies.append(pltpu.make_async_copy(held.at[:, at], out.at[:, at], sems.at[i]))
            copies[-1].start()
        for copy in copies:
            copy.wait()

    return pl.pallas_call(
        kernel,
        out_shape=jax.ShapeDtypeStruct((features, width), BF),
        in_specs=[pl.BlockSpec(memory_space=pltpu.VMEM)] * 2,
        out_specs=pl.BlockSpec(memory_space=pltpu.HBM),
        scratch_shapes=[
            pltpu.VMEM((features, width), BF),
            pltpu.SemaphoreType.DMA((count,)),
        ],
        compiler_params=pltpu.CompilerParams(vmem_limit_bytes=32 << 20),
        name="product",
    )(local, cot)


def after(value, other):
    return lax.optimization_barrier((value, other))[0]


def halve(tokens, weight, to_half, to_quarter):
    full = matmul(tokens, weight)
    away = full[64:].astype(BF)
    half = full[:64] + send(away, to_half)
    return half[:32] + send(half[32:].astype(BF), to_quarter), away


def scatter_second(quarter):
    got = [send(quarter[:, 8 * e : 8 * e + 8].astype(BF), second_shift(e)) for e in (2, 1, 3)]
    return quarter[:, :8] + got[0] + got[1] + got[2]


def scatter_first(full):
    got = [send(full[:, 32 * d : 32 * d + 32].astype(BF), first_shift(d)) for d in (2, 1, 3)]
    return full[:, :32] + got[0] + got[1] + got[2]


def sum_second(part):
    rounded = part.astype(BF)
    for e in (2, 1, 3):
        part = part + jnp.roll(send(rounded, second_shift(e)), -8 * e, axis=0)
    return part


def gather_second(own):
    got = {e: send(own, second_shift(-e)) for e in (2, 1, 3)}
    return jnp.concatenate([own, got[1], got[2], got[3]], axis=1)


def gather_second_pairs(own, next_, even):
    both = send(jnp.concatenate([own, next_], axis=1), along_second(far))
    before, across = both[:, :8], both[:, 8:]
    return jnp.concatenate(
        [own, jnp.where(even, next_, before), across, jnp.where(even, before, next_)], axis=1
    )


def gather_first(own):
    got = {d: send(own, first_shift(-d)) for d in (2, 1, 3)}
    return jnp.concatenate([own, got[1], got[2], got[3]], axis=1)


def swap_axes(value):
    return value.reshape(4, 4, 8, -1).swapaxes(0, 1).reshape(value.shape)


def sum_rows(part, factors, next_, k, even):
    rounded = part.astype(BF)
    got = [send(rounded, z_shift(d)) for d in (1, 3, 2)]
    factors = gather_second_pairs(factors, after(next_, part), even)
    chips = part + got[0] + got[1] + got[2]
    return chips + swap_axes(send(chips, CORE)), factors[0], factors[1]


def body(tokens, gate_weight, up_weight, down_weight, gate_tangent, up_tangent):
    row, col = lax.axis_index("row"), lax.axis_index("col")
    z, k, y, x = row // 2, row % 2, col // 4, col % 4
    even = jnp.where(k == 0, y, x) & 1 == 0
    out_scale = 128.0 ** (-0.5)
    gate_weight = into_vmem(gate_weight)
    own, other = gather_tokens(tokens, gate_weight)
    turn = 1 - 2 * (jnp.where(k == 0, x, y) & 1)

    def ordered(*offsets):
        picked = order_matrix(offsets, z, k, x, y)
        return (matmul(picked[:, :64], own) + matmul(picked[:, 64:], other)).astype(BF)

    ahead, behind = ordered(0, -turn, turn, 2), ordered(0, turn, -turn, 2)
    local = ordered(0, 1, 2, 3)
    near_far = along_first(near), along_first(far)
    far_near = along_first(far), along_first(near)
    gate_sum, sent = halve(ahead, gate_weight, *near_far)
    up_sum, sent = halve(after(behind, sent), up_weight, *far_near)
    gate_dir, sent = halve(after(ahead, sent), gate_tangent, *near_far)
    up_dir, sent = halve(after(behind, sent), up_tangent, *far_near)
    gate_sum, up_sum, gate_dir, up_dir = scatter_second(
        jnp.stack([gate_sum, up_sum, gate_dir, up_dir])
    )
    sigmoid = jax.nn.sigmoid(gate_sum)
    activated = gate_sum * sigmoid
    up_slopes = up_sum * (sigmoid * (1.0 + gate_sum * (1.0 - sigmoid)))
    hidden = (up_slopes * gate_dir + activated * up_dir).astype(BF)

    factors = jnp.stack([up_slopes, activated]).astype(BF)
    hidden = gather_second(hidden[None])
    next_ = send(after(factors, hidden), along_second(near))
    hidden = after(gather_first(hidden)[0], next_)
    half, up_slopes, activated = sum_rows(matmul(hidden, down_weight), factors, next_, k, even)
    output_dir = (half * out_scale).astype(BF)
    back = sum_second(scatter_first(against_rows(output_dir, down_weight)[None])[0])
    gate_cot = gather_first((back * up_slopes).astype(BF)[None])[0]
    up_cot = gather_first((back * activated).astype(BF)[None])[0]
    return product(local, gate_cot), product(local, up_cot)


def solution(mesh):
    placed = (
        P("row", "col"),
        P("col", "row"),
        P("col", "row"),
        P("row", "col"),
        P("col", "row"),
        P("col", "row"),
    )
    return jax.shard_map(
        body,
        mesh=mesh,
        in_specs=placed,
        out_specs=(P("col", "row"), P("col", "row")),
        check_vma=False,
    )
```

```python
import jax
import jax.numpy as jnp
from jax import lax
from jax.experimental import pallas as pl
from jax.experimental.pallas import tpu as pltpu
from jax.sharding import PartitionSpec as P

BF = jnp.bfloat16
F32 = jnp.float32
RC = ("row", "col")


def device(z, k, y, x):
    return ((z % 4) * 2 + k) * 16 + (y % 4) * 4 + (x % 4)


def pairs(move):
    return [
        (device(z, k, y, x), device(*move(z, k, y, x)))
        for z in range(4)
        for k in range(2)
        for y in range(4)
        for x in range(4)
    ]


def near(i):
    return i ^ 1


def far(i):
    return i + 1 if i % 2 else i - 1


def along_first(move):
    return pairs(lambda z, k, y, x: (z, k, y, move(x)) if k == 0 else (z, k, move(y), x))


def along_second(move):
    return pairs(lambda z, k, y, x: (z, k, move(y), x) if k == 0 else (z, k, y, move(x)))


CORE = pairs(lambda z, k, y, x: (z, 1 - k, y, x))


def z_shift(d):
    return pairs(lambda z, k, y, x: (z + d, k, y, x))


def first_shift(d):
    return along_first(lambda i: i + d)


def second_shift(d):
    return along_second(lambda i: i + d)


def send(value, to):
    return lax.ppermute(value, RC, to)


def matmul(left, right):
    return jnp.dot(left, right, preferred_element_type=F32)


def gather_tokens(tokens, ready):
    got = {d: send(tokens, z_shift(d)) for d in (2, 1, 3)}
    own = jnp.concatenate([tokens, got[1], got[2], got[3]])
    own = after(own, ready)
    return own, send(own, CORE)


def order_matrix(offsets, z, k, x, y):
    local = lax.broadcasted_iota(jnp.int32, (128, 128), 0)
    column = lax.broadcasted_iota(jnp.int32, (128, 128), 1)
    block, second = local // 32, local // 8 % 4
    first = jnp.where(
        block == 1, offsets[1], jnp.where(block == 2, offsets[2], jnp.where(block == 3, offsets[3], offsets[0]))
    )
    high = (x + jnp.where(k == 0, first, second)) & 3
    low = (y + jnp.where(k == 0, second, first)) & 3
    token = (high * 4 + low) * 8 + local % 8
    place = ((token // 16 & 1) ^ k) * 64 + ((z - token // 32) & 3) * 16 + token % 16
    return (place == column).astype(BF)


def into_vmem(array):
    rows, width = array.shape
    cut = 4

    def kernel(source, target, sems):
        copies = [
            pltpu.make_async_copy(
                source.at[pl.ds(i * rows // cut, rows // cut)],
                target.at[pl.ds(i * rows // cut, rows // cut)],
                sems.at[i],
            )
            for i in range(cut)
        ]
        for copy in copies:
            copy.start()
        for copy in copies:
            copy.wait()

    return pl.pallas_call(
        kernel,
        out_shape=jax.ShapeDtypeStruct(array.shape, array.dtype),
        in_specs=[pl.BlockSpec(memory_space=pltpu.HBM)],
        out_specs=pl.BlockSpec(memory_space=pltpu.VMEM),
        scratch_shapes=[pltpu.SemaphoreType.DMA((cut,))],
        compiler_params=pltpu.CompilerParams(vmem_limit_bytes=32 << 20),
        cost_estimate=pl.CostEstimate(
            flops=0, bytes_accessed=array.size * 2, transcendentals=0
        ),
        name="into_vmem",
    )(array)


def product(local, cot):
    features, width = local.shape[1], cot.shape[1]
    step = 256
    count = width // step

    def kernel(local_ref, cot_ref, out, held, sems):
        left = local_ref[...].T
        copies = []
        for i in range(count):
            at = pl.ds(i * step, step)
            held[:, at] = matmul(left, cot_ref[:, at]).astype(BF)
            copies.append(pltpu.make_async_copy(held.at[:, at], out.at[:, at], sems.at[i]))
            copies[-1].start()
        for copy in copies:
            copy.wait()

    return pl.pallas_call(
        kernel,
        out_shape=jax.ShapeDtypeStruct((features, width), BF),
        in_specs=[pl.BlockSpec(memory_space=pltpu.VMEM)] * 2,
        out_specs=pl.BlockSpec(memory_space=pltpu.HBM),
        scratch_shapes=[
            pltpu.VMEM((features, width), BF),
            pltpu.SemaphoreType.DMA((count,)),
        ],
        compiler_params=pltpu.CompilerParams(vmem_limit_bytes=32 << 20),
        name="product",
    )(local, cot)


def after(value, other):
    return lax.optimization_barrier((value, other))[0]


def halve(tokens, weight, to_half, to_quarter):
    full = matmul(tokens, weight)
    away = full[64:].astype(BF)
    half = full[:64] + send(away, to_half)
    return half[:32] + send(half[32:].astype(BF), to_quarter), away


def scatter_second(quarter):
    got = [send(quarter[:, 8 * e : 8 * e + 8].astype(BF), second_shift(e)) for e in (2, 1, 3)]
    return quarter[:, :8] + got[0] + got[1] + got[2]


def scatter_first(full):
    got = [send(full[:, 32 * d : 32 * d + 32].astype(BF), first_shift(d)) for d in (2, 1, 3)]
    return full[:, :32] + got[0] + got[1] + got[2]


def sum_second(part):
    rounded = part.astype(BF)
    for e in (2, 1, 3):
        part = part + jnp.roll(send(rounded, second_shift(e)), -8 * e, axis=0)
    return part


def gather_second(own):
    got = {e: send(own, second_shift(-e)) for e in (2, 1, 3)}
    return jnp.concatenate([own, got[1], got[2], got[3]], axis=1)


def gather_second_pairs(own, next_, even):
    both = send(jnp.concatenate([own, next_], axis=1), along_second(far))
    before, across = both[:, :8], both[:, 8:]
    return jnp.concatenate(
        [own, jnp.where(even, next_, before), across, jnp.where(even, before, next_)], axis=1
    )


def gather_first(own):
    got = {d: send(own, first_shift(-d)) for d in (2, 1, 3)}
    return jnp.concatenate([own, got[1], got[2], got[3]], axis=1)


def swap_axes(value):
    return value.reshape(4, 4, 8, -1).swapaxes(0, 1).reshape(value.shape)


def sum_rows(part, factors, next_, even):
    rounded = part.astype(BF)
    got = [send(rounded, z_shift(d)) for d in (1, 3, 2)]
    factors = gather_second_pairs(factors, after(next_, part), even)
    chips = part + got[0] + got[1] + got[2]
    return chips + swap_axes(send(chips, CORE)), factors[0], factors[1]


def body(tokens, gate_weight, up_weight, down_weight, gate_tangent, up_tangent):
    row, col = lax.axis_index("row"), lax.axis_index("col")
    z, k, y, x = row // 2, row % 2, col // 4, col % 4
    even = jnp.where(k == 0, y, x) & 1 == 0
    out_scale = 128.0 ** (-0.5)
    gate_weight = into_vmem(gate_weight)
    own, other = gather_tokens(tokens, gate_weight)
    turn = 1 - 2 * (jnp.where(k == 0, x, y) & 1)

    def ordered(*offsets):
        picked = order_matrix(offsets, z, k, x, y)
        return (matmul(picked[:, :64], own) + matmul(picked[:, 64:], other)).astype(BF)

    ahead, behind = ordered(0, -turn, turn, 2), ordered(0, turn, -turn, 2)
    local = ordered(0, 1, 2, 3)
    near_far = along_first(near), along_first(far)
    far_near = along_first(far), along_first(near)
    gate_sum, sent = halve(ahead, gate_weight, *near_far)
    up_sum, sent = halve(after(behind, sent), up_weight, *far_near)
    gate_dir, sent = halve(after(ahead, sent), gate_tangent, *near_far)
    up_dir, sent = halve(after(behind, sent), up_tangent, *far_near)
    down_t = lax.optimization_barrier(after(down_weight, sent).T)
    gate_dir = after(gate_dir, down_t)
    gate_sum, up_sum, gate_dir, up_dir = scatter_second(
        jnp.stack([gate_sum, up_sum, gate_dir, up_dir])
    )
    sigmoid = jax.nn.sigmoid(gate_sum)
    activated = gate_sum * sigmoid
    up_slopes = up_sum * (sigmoid * (1.0 + gate_sum * (1.0 - sigmoid)))
    hidden = (up_slopes * gate_dir + activated * up_dir).astype(BF)

    factors = jnp.stack([up_slopes, activated]).astype(BF)
    hidden = gather_second(hidden[None])
    next_ = send(after(factors, hidden), along_second(near))
    hidden = after(gather_first(hidden)[0], next_)
    half, up_slopes, activated = sum_rows(matmul(hidden, down_weight), factors, next_, even)
    output_dir = (half * out_scale).astype(BF)
    back = sum_second(scatter_first(matmul(output_dir, down_t)[None])[0])
    gate_cot = gather_first((back * up_slopes).astype(BF)[None])[0]
    up_cot = gather_first((back * activated).astype(BF)[None])[0]
    return product(local, gate_cot), product(local, up_cot)


def solution(mesh):
    placed = (
        P("row", "col"),
        P("col", "row"),
        P("col", "row"),
        P("row", "col"),
        P("col", "row"),
        P("col", "row"),
    )
    return jax.shard_map(
        body,
        mesh=mesh,
        in_specs=placed,
        out_specs=(P("col", "row"), P("col", "row")),
        check_vma=False,
    )
```

```python
import jax
import jax.numpy as jnp
from jax import lax
from jax.experimental import pallas as pl
from jax.experimental.pallas import tpu as pltpu
from jax.sharding import PartitionSpec as P

BF = jnp.bfloat16
F32 = jnp.float32
RC = ("row", "col")


def device(z, k, y, x):
    return ((z % 4) * 2 + k) * 16 + (y % 4) * 4 + (x % 4)


def pairs(move):
    return [
        (device(z, k, y, x), device(*move(z, k, y, x)))
        for z in range(4)
        for k in range(2)
        for y in range(4)
        for x in range(4)
    ]


def near(i):
    return i ^ 1


def far(i):
    return i + 1 if i % 2 else i - 1


def along_first(move):
    return pairs(lambda z, k, y, x: (z, k, y, move(x)) if k == 0 else (z, k, -move(-y & 3), x))


def along_second(move):
    return pairs(lambda z, k, y, x: (z, k, move(y), x) if k == 0 else (z, k, y, -move(-x & 3)))


CORE = pairs(lambda z, k, y, x: (z, 1 - k, y, x))


def z_shift(d):
    return pairs(lambda z, k, y, x: (z + d, k, y, x))


def first_shift(d):
    return along_first(lambda i: i + d)


def second_shift(d):
    return along_second(lambda i: i + d)


def send(value, to):
    return lax.ppermute(value, RC, to)


def matmul(left, right):
    return jnp.dot(left, right, preferred_element_type=F32)


def gather_tokens(tokens, ready):
    got = {d: send(tokens, z_shift(d)) for d in (2, 1, 3)}
    own = jnp.concatenate([tokens, got[1], got[2], got[3]])
    own = after(own, ready)
    return own, send(own, CORE)


def order_matrix(offsets, z, k, x, y):
    local = lax.broadcasted_iota(jnp.int32, (128, 128), 0)
    column = lax.broadcasted_iota(jnp.int32, (128, 128), 1)
    block, second = local // 32, local // 8 % 4
    first = jnp.where(
        block == 1, offsets[1], jnp.where(block == 2, offsets[2], jnp.where(block == 3, offsets[3], offsets[0]))
    )
    high = (x + jnp.where(k == 0, first, -second)) & 3
    low = (y + jnp.where(k == 0, second, -first)) & 3
    token = (high * 4 + low) * 8 + local % 8
    place = ((token // 16 & 1) ^ k) * 64 + ((z - token // 32) & 3) * 16 + token % 16
    return (place == column).astype(BF)


def into_vmem(array):
    rows, width = array.shape
    cut = 4

    def kernel(source, target, sems):
        copies = [
            pltpu.make_async_copy(
                source.at[pl.ds(i * rows // cut, rows // cut)],
                target.at[pl.ds(i * rows // cut, rows // cut)],
                sems.at[i],
            )
            for i in range(cut)
        ]
        for copy in copies:
            copy.start()
        for copy in copies:
            copy.wait()

    return pl.pallas_call(
        kernel,
        out_shape=jax.ShapeDtypeStruct(array.shape, array.dtype),
        in_specs=[pl.BlockSpec(memory_space=pltpu.HBM)],
        out_specs=pl.BlockSpec(memory_space=pltpu.VMEM),
        scratch_shapes=[pltpu.SemaphoreType.DMA((cut,))],
        compiler_params=pltpu.CompilerParams(vmem_limit_bytes=32 << 20),
        cost_estimate=pl.CostEstimate(
            flops=0, bytes_accessed=array.size * 2, transcendentals=0
        ),
        name="into_vmem",
    )(array)


def product(local, cot):
    features, width = local.shape[1], cot.shape[1]
    step = 256
    count = width // step

    def kernel(local_ref, cot_ref, out, held, sems):
        left = local_ref[...].T
        copies = []
        for i in range(count):
            at = pl.ds(i * step, step)
            held[:, at] = matmul(left, cot_ref[:, at]).astype(BF)
            copies.append(pltpu.make_async_copy(held.at[:, at], out.at[:, at], sems.at[i]))
            copies[-1].start()
        for copy in copies:
            copy.wait()

    return pl.pallas_call(
        kernel,
        out_shape=jax.ShapeDtypeStruct((features, width), BF),
        in_specs=[pl.BlockSpec(memory_space=pltpu.VMEM)] * 2,
        out_specs=pl.BlockSpec(memory_space=pltpu.HBM),
        scratch_shapes=[
            pltpu.VMEM((features, width), BF),
            pltpu.SemaphoreType.DMA((count,)),
        ],
        compiler_params=pltpu.CompilerParams(vmem_limit_bytes=32 << 20),
        name="product",
    )(local, cot)


def after(value, other):
    return lax.optimization_barrier((value, other))[0]


def halve(tokens, weight, to_half, to_quarter):
    full = matmul(tokens, weight)
    away = full[64:].astype(BF)
    half = full[:64] + send(away, to_half)
    return half[:32] + send(half[32:].astype(BF), to_quarter), away


def scatter_second(quarter):
    got = [send(quarter[:, 8 * e : 8 * e + 8].astype(BF), second_shift(e)) for e in (2, 1, 3)]
    return quarter[:, :8] + got[0] + got[1] + got[2]


def scatter_first(full):
    got = [send(full[:, 32 * d : 32 * d + 32].astype(BF), first_shift(d)) for d in (2, 1, 3)]
    return full[:, :32] + got[0] + got[1] + got[2]


def sum_second(part):
    rounded = part.astype(BF)
    for e in (2, 1, 3):
        part = part + jnp.roll(send(rounded, second_shift(e)), -8 * e, axis=0)
    return part


def gather_second(own):
    got = {e: send(own, second_shift(-e)) for e in (2, 1, 3)}
    return jnp.concatenate([own, got[1], got[2], got[3]], axis=1)


def gather_second_pairs(own, next_, even):
    both = send(jnp.concatenate([own, next_], axis=1), along_second(far))
    before, across = both[:, :8], both[:, 8:]
    return jnp.concatenate(
        [own, jnp.where(even, next_, before), across, jnp.where(even, before, next_)], axis=1
    )


def gather_first(own):
    got = {d: send(own, first_shift(-d)) for d in (2, 1, 3)}
    return jnp.concatenate([own, got[1], got[2], got[3]], axis=1)


def swap_axes(value):
    blocks = value.reshape(4, 4, 8, -1)
    back = (0, 3, 2, 1)
    return jnp.concatenate([blocks[i, j] for j in back for i in back])


def sum_rows(part, factors, next_, even):
    rounded = part.astype(BF)
    got = [send(rounded, z_shift(d)) for d in (1, 3, 2)]
    factors = gather_second_pairs(factors, after(next_, part), even)
    chips = part + got[0] + got[1] + got[2]
    return chips + swap_axes(send(chips.astype(BF), CORE)), factors[0], factors[1]


def body(tokens, gate_weight, up_weight, down_weight, gate_tangent, up_tangent):
    row, col = lax.axis_index("row"), lax.axis_index("col")
    z, k, y, x = row // 2, row % 2, col // 4, col % 4
    even = jnp.where(k == 0, y, x) & 1 == 0
    out_scale = 128.0 ** (-0.5)
    gate_weight = into_vmem(gate_weight)
    own, other = gather_tokens(tokens, gate_weight)
    turn = 1 - 2 * (jnp.where(k == 0, x, y) & 1)

    def ordered(*offsets):
        picked = order_matrix(offsets, z, k, x, y)
        return (matmul(picked[:, :64], own) + matmul(picked[:, 64:], other)).astype(BF)

    ahead, behind = ordered(0, -turn, turn, 2), ordered(0, turn, -turn, 2)
    local = ordered(0, 1, 2, 3)
    near_far = along_first(near), along_first(far)
    far_near = along_first(far), along_first(near)
    gate_sum, sent = halve(ahead, gate_weight, *near_far)
    up_sum, sent = halve(after(behind, sent), up_weight, *far_near)
    gate_dir, sent = halve(after(ahead, sent), gate_tangent, *near_far)
    up_dir, sent = halve(after(behind, sent), up_tangent, *far_near)
    down_t = lax.optimization_barrier(after(down_weight, sent).T)
    gate_dir = after(gate_dir, down_t)
    gate_sum, up_sum, gate_dir, up_dir = scatter_second(
        jnp.stack([gate_sum, up_sum, gate_dir, up_dir])
    )
    sigmoid = jax.nn.sigmoid(gate_sum)
    activated = gate_sum * sigmoid
    up_slopes = up_sum * (sigmoid * (1.0 + gate_sum * (1.0 - sigmoid)))
    hidden = (up_slopes * gate_dir + activated * up_dir).astype(BF)

    factors = jnp.stack([up_slopes, activated]).astype(BF)
    hidden = gather_second(hidden[None])
    next_ = send(after(factors, hidden), along_second(near))
    hidden = after(gather_first(hidden)[0], next_)
    half, up_slopes, activated = sum_rows(matmul(hidden, down_weight), factors, next_, even)
    output_dir = (half * out_scale).astype(BF)
    back = sum_second(scatter_first(matmul(output_dir, down_t)[None])[0])
    gate_cot = gather_first((back * up_slopes).astype(BF)[None])[0]
    up_cot = gather_first((back * activated).astype(BF)[None])[0]
    return product(local, gate_cot), product(local, up_cot)


def solution(mesh):
    placed = (
        P("row", "col"),
        P("col", "row"),
        P("col", "row"),
        P("row", "col"),
        P("col", "row"),
        P("col", "row"),
    )
    return jax.shard_map(
        body,
        mesh=mesh,
        in_specs=placed,
        out_specs=(P("col", "row"), P("col", "row")),
        check_vma=False,
    )
```

```python
import jax
import jax.numpy as jnp
from jax import lax
from jax.experimental import pallas as pl
from jax.experimental.pallas import tpu as pltpu
from jax.sharding import PartitionSpec as P

BF = jnp.bfloat16
F32 = jnp.float32
RC = ("row", "col")


def device(z, k, y, x):
    return ((z % 4) * 2 + k) * 16 + (y % 4) * 4 + (x % 4)


def pairs(move):
    return [
        (device(z, k, y, x), device(*move(z, k, y, x)))
        for z in range(4)
        for k in range(2)
        for y in range(4)
        for x in range(4)
    ]


def near(i):
    return i ^ 1


def far(i):
    return i + 1 if i % 2 else i - 1


def along_first(move):
    return pairs(lambda z, k, y, x: (z, k, y, move(x)) if k == 0 else (z, k, -move(-y & 3), x))


def along_second(move):
    return pairs(lambda z, k, y, x: (z, k, move(y), x) if k == 0 else (z, k, y, -move(-x & 3)))


CORE = pairs(lambda z, k, y, x: (z, 1 - k, y, x))


def z_shift(d):
    return pairs(lambda z, k, y, x: (z + d, k, y, x))


def first_shift(d):
    return along_first(lambda i: i + d)


def second_shift(d):
    return along_second(lambda i: i + d)


def send(value, to):
    return lax.ppermute(value, RC, to)


def matmul(left, right):
    return jnp.dot(left, right, preferred_element_type=F32)


def gather_tokens(tokens, ready):
    got = {d: send(tokens, z_shift(d)) for d in (2, 1, 3)}
    own = jnp.concatenate([tokens, got[1], got[2], got[3]])
    own = after(own, ready)
    return own, send(own, CORE)


def order_matrix(offsets, z, k, x, y):
    local = lax.broadcasted_iota(jnp.int32, (128, 128), 0)
    column = lax.broadcasted_iota(jnp.int32, (128, 128), 1)
    block, second = local // 32, local // 8 % 4
    first = jnp.where(
        block == 1, offsets[1], jnp.where(block == 2, offsets[2], jnp.where(block == 3, offsets[3], offsets[0]))
    )
    high = (x + jnp.where(k == 0, first, -second)) & 3
    low = (y + jnp.where(k == 0, second, -first)) & 3
    token = (high * 4 + low) * 8 + local % 8
    place = ((token // 16 & 1) ^ k) * 64 + ((z - token // 32) & 3) * 16 + token % 16
    return (place == column).astype(BF)


def into_vmem(array):
    rows, width = array.shape
    cut = 4

    def kernel(source, target, sems):
        copies = [
            pltpu.make_async_copy(
                source.at[pl.ds(i * rows // cut, rows // cut)],
                target.at[pl.ds(i * rows // cut, rows // cut)],
                sems.at[i],
            )
            for i in range(cut)
        ]
        for copy in copies:
            copy.start()
        for copy in copies:
            copy.wait()

    return pl.pallas_call(
        kernel,
        out_shape=jax.ShapeDtypeStruct(array.shape, array.dtype),
        in_specs=[pl.BlockSpec(memory_space=pltpu.HBM)],
        out_specs=pl.BlockSpec(memory_space=pltpu.VMEM),
        scratch_shapes=[pltpu.SemaphoreType.DMA((cut,))],
        compiler_params=pltpu.CompilerParams(vmem_limit_bytes=32 << 20),
        cost_estimate=pl.CostEstimate(
            flops=0, bytes_accessed=array.size * 2, transcendentals=0
        ),
        name="into_vmem",
    )(array)


def product(local, cot):
    features, width = local.shape[1], cot.shape[1]
    step = 256
    count = width // step

    def kernel(local_ref, cot_ref, out, held, sems):
        left = local_ref[...].T
        copies = []
        for i in range(count):
            at = pl.ds(i * step, step)
            held[:, at] = matmul(left, cot_ref[:, at]).astype(BF)
            copies.append(pltpu.make_async_copy(held.at[:, at], out.at[:, at], sems.at[i]))
            copies[-1].start()
        for copy in copies:
            copy.wait()

    return pl.pallas_call(
        kernel,
        out_shape=jax.ShapeDtypeStruct((features, width), BF),
        in_specs=[pl.BlockSpec(memory_space=pltpu.VMEM)] * 2,
        out_specs=pl.BlockSpec(memory_space=pltpu.HBM),
        scratch_shapes=[
            pltpu.VMEM((features, width), BF),
            pltpu.SemaphoreType.DMA((count,)),
        ],
        compiler_params=pltpu.CompilerParams(vmem_limit_bytes=32 << 20),
        name="product",
    )(local, cot)


def after(value, other):
    return lax.optimization_barrier((value, other))[0]


def halve(tokens, weight, to_half, to_quarter):
    full = matmul(tokens, weight)
    away = full[64:].astype(BF)
    half = full[:64] + send(away, to_half)
    return half[:32] + send(half[32:].astype(BF), to_quarter), away


def scatter_second(quarter):
    got = [send(quarter[:, 8 * e : 8 * e + 8].astype(BF), second_shift(e)) for e in (2, 1, 3)]
    return quarter[:, :8] + got[0] + got[1] + got[2]


def scatter_first(full):
    got = [send(full[:, 32 * d : 32 * d + 32].astype(BF), first_shift(d)) for d in (2, 1, 3)]
    return full[:, :32] + got[0] + got[1] + got[2]


def sum_second(part):
    rounded = part.astype(BF)
    got = [jnp.roll(send(rounded, second_shift(e)), -8 * e, axis=0) for e in (2, 1, 3)]
    return part + got[0] + got[1] + got[2]


def gather_second(own):
    got = {e: send(own, second_shift(-e)) for e in (2, 1, 3)}
    return jnp.concatenate([own, got[1], got[2], got[3]], axis=1)


def gather_second_pairs(own, next_, even):
    both = send(jnp.concatenate([own, next_], axis=1), along_second(far))
    before, across = both[:, :8], both[:, 8:]
    return jnp.concatenate(
        [own, jnp.where(even, next_, before), across, jnp.where(even, before, next_)], axis=1
    )


def gather_first(own):
    got = {d: send(own, first_shift(-d)) for d in (2, 1, 3)}
    return jnp.concatenate([own, got[1], got[2], got[3]], axis=1)


def swap_axes(value):
    blocks = value.reshape(4, 4, 8, -1)
    back = (0, 3, 2, 1)
    return jnp.concatenate([blocks[i, j] for j in back for i in back])


def sum_rows(part, factors, next_, even):
    rounded = part.astype(BF)
    got = [send(rounded, z_shift(d)) for d in (1, 3, 2)]
    factors = gather_second_pairs(factors, after(next_, part), even)
    chips = part + got[0] + got[1] + got[2]
    return chips + swap_axes(send(chips.astype(BF), CORE)), factors[0], factors[1]


def body(tokens, gate_weight, up_weight, down_weight, gate_tangent, up_tangent):
    row, col = lax.axis_index("row"), lax.axis_index("col")
    z, k, y, x = row // 2, row % 2, col // 4, col % 4
    even = jnp.where(k == 0, y, x) & 1 == 0
    out_scale = 128.0 ** (-0.5)
    gate_weight = into_vmem(gate_weight)
    own, other = gather_tokens(tokens, gate_weight)
    turn = 1 - 2 * (jnp.where(k == 0, x, y) & 1)

    def ordered(*offsets):
        picked = order_matrix(offsets, z, k, x, y)
        return (matmul(picked[:, :64], own) + matmul(picked[:, 64:], other)).astype(BF)

    ahead, behind = ordered(0, -turn, turn, 2), ordered(0, turn, -turn, 2)
    local = ordered(0, 1, 2, 3)
    near_far = along_first(near), along_first(far)
    far_near = along_first(far), along_first(near)
    gate_sum, sent = halve(ahead, gate_weight, *near_far)
    up_sum, sent = halve(after(behind, sent), up_weight, *far_near)
    gate_dir, sent = halve(after(ahead, sent), gate_tangent, *near_far)
    up_dir, sent = halve(after(behind, sent), up_tangent, *far_near)
    down_t = lax.optimization_barrier(after(down_weight, sent).T)
    gate_dir = after(gate_dir, down_t)
    gate_sum, up_sum, gate_dir, up_dir = scatter_second(
        jnp.stack([gate_sum, up_sum, gate_dir, up_dir])
    )
    sigmoid = jax.nn.sigmoid(gate_sum)
    activated = gate_sum * sigmoid
    up_slopes = up_sum * (sigmoid * (1.0 + gate_sum * (1.0 - sigmoid)))
    hidden = (up_slopes * gate_dir + activated * up_dir).astype(BF)

    factors = jnp.stack([up_slopes, activated]).astype(BF)
    hidden = gather_second(hidden[None])
    next_ = send(after(factors, hidden), along_second(near))
    hidden = after(gather_first(hidden)[0], next_)
    half, up_slopes, activated = sum_rows(matmul(hidden, down_weight), factors, next_, even)
    output_dir = (half * out_scale).astype(BF)
    back = sum_second(scatter_first(matmul(output_dir, down_t)[None])[0])
    gate_cot = gather_first((back * up_slopes).astype(BF)[None])[0]
    up_cot = gather_first((back * activated).astype(BF)[None])[0]
    return product(local, gate_cot), product(local, up_cot)


def solution(mesh):
    placed = (
        P("row", "col"),
        P("col", "row"),
        P("col", "row"),
        P("row", "col"),
        P("col", "row"),
        P("col", "row"),
    )
    return jax.shard_map(
        body,
        mesh=mesh,
        in_specs=placed,
        out_specs=(P("col", "row"), P("col", "row")),
        check_vma=False,
    )
```
